32 devices in a mesh: dp: 4 (over x, core), ctx: 8 (over z, y).
Axes of the slice: x: 2, y: 2, z: 4, core: 2. Of those that a mesh axis runs over, the one named last changes fastest.
Arguments:
- tokens_in: bfloat16 [4, 2048, 960], P('dp', 'ctx'), may hold values from -6 to 6
- cotangent: bfloat16 [4, 2048, 960], P('dp', 'ctx'), may hold values from -6 to 6
- w_query: bfloat16 [921600], P(('dp', 'ctx')), may hold values from -0.25 to 0.25
- w_key: bfloat16 [307200], P(('dp', 'ctx')), may hold values from -0.25 to 0.25
- w_value: bfloat16 [307200], P(('dp', 'ctx')), may hold values from -0.1875 to 0.1875
- w_output: bfloat16 [921600], P(('dp', 'ctx')), may hold values from -0.75 to 0.75
- w_gate: bfloat16 [2457600], P(('dp', 'ctx')), may hold values from -0.1875 to 0.1875
- w_up: bfloat16 [2457600], P(('dp', 'ctx')), may hold values from -0.1875 to 0.1875
- w_down: bfloat16 [2457600], P(('dp', 'ctx')), may hold values from -0.15625 to 0.15625
- norm_gains: bfloat16 [2, 960], replicated, may hold values from 0.25 to 1.75
- seq_lengths: int32 [4, 3], P('dp'), may hold values from 32 to 1920, as said below
- block_order: int32 [4, 16], P('dp'), may hold values from 0 to 15, as said below
Outputs:
- block_out: float32 [4, 2048, 960], P('dp', 'ctx')
- grad_input: float32 [4, 2048, 960], P('dp', 'ctx')
- grad_query: float32 [921600], P(('dp', 'ctx'))
- grad_key: float32 [307200], P(('dp', 'ctx'))
- grad_value: float32 [307200], P(('dp', 'ctx'))
- grad_output: float32 [921600], P(('dp', 'ctx'))
- grad_gate: float32 [2457600], P(('dp', 'ctx'))
- grad_up: float32 [2457600], P(('dp', 'ctx'))
- grad_down: float32 [2457600], P(('dp', 'ctx'))
- grad_gains: float32 [2, 960], replicated
The draws below stay inside these ranges and needn't reach their ends.
Inputs may be any that keep to these rules, and one draw needn't show every extreme that they name: `seq_lengths`: each group has one document, at a place drawn from the seed, of 1920 tokens; the other two together have 128 tokens. `block_order`: each row is a permutation of the group's blocks; the first stored block of the first device of ctx, the first stored block of the device at index 4 of ctx, and the last stored block of the last device of ctx hold the packed blocks second, third and fourth from the end.
All inputs are finite; a program needn't handle non-finite values.
Results may differ from the reference program's by a relative error of at most 0.018.
Values may be sent and summed in bfloat16 or wider, within the bound.
A program may use at most 256 MiB of HBM per device.

```python
import jax
import jax.numpy as jnp
from jax import lax

D = 960
HEADS = 15
KV_HEADS = 5
HEAD_DIM = 64
FF = 2560
BLOCK = 128
SEQS = 3
BLK_DEV = 2
BLOCKS = 16
GROUP_TOK = 2048
GROUPS = 4
Q_WIDTH = 960
KV_WIDTH = 320
N_CTX = 8


def draw_seq_lengths(key, part):
    key = jax.random.fold_in(key, 3)
    first_key, place_key = jax.random.split(key)
    short_one = jax.random.randint(first_key, (GROUPS,), BLOCK // 4, 3 * BLOCK // 4 + 1)
    short_two = BLOCK - short_one
    long_place = jax.random.randint(place_key, (GROUPS,), 0, SEQS)
    column = jnp.arange(SEQS, dtype=jnp.int32)[None, :]
    ranked = column - (column > long_place[:, None]).astype(jnp.int32)
    shorts = jnp.where(ranked == 0, short_one[:, None], short_two[:, None])
    return jnp.where(column == long_place[:, None], GROUP_TOK - BLOCK, shorts).astype(jnp.int32)


def draw_block_order(key, part):
    key = jax.random.fold_in(key, 5)
    group_keys = jax.random.split(key, GROUPS)
    middle = BLK_DEV * (N_CTX // 2)

    def one_group(group_key):
        arrangement = jax.random.permutation(group_key, BLOCKS).astype(jnp.int32)
        for target, block_id in ((0, BLOCKS - 2), (middle, BLOCKS - 3), (BLOCKS - 1, BLOCKS - 4)):
            where_now = jnp.argmax(arrangement == block_id)
            current = arrangement[target]
            arrangement = arrangement.at[where_now].set(current).at[target].set(block_id)
        return arrangement
    return jax.vmap(one_group)(group_keys).astype(jnp.int32)


def steps_of(own_key, dims, pieces, low, high):
    def one(dim, blocks):
        draws = jax.random.uniform(jax.random.fold_in(jax.random.fold_in(own_key, 6), dim), (blocks,), jnp.float32, low / len(pieces), high / len(pieces))
        return jnp.repeat(jnp.exp(draws), dims[dim] // blocks).reshape((-1,) + (1,) * (len(dims) - dim - 1))

    level = one(*pieces[0])
    for cut in pieces[1:]:
        level = level * one(*cut)
    return level


def centred(key, shape, spread, bound, shards=(), kind=jnp.bfloat16):
    level = steps_of(key, shape, shards, -0.22, 0.18) if shards else 1.0
    entries = jax.random.normal(key, shape, jnp.float32) * spread * level
    return jnp.minimum(jnp.maximum(entries, -bound), bound).astype(kind)


def setup_inputs(seed: int = 0) -> dict:
    key_of = jax.random.split(jax.random.key(seed), 13)
    return {
        "tokens_in": centred(key_of[0], (GROUPS, GROUP_TOK, D), 1.0, 6.0, ((0, 4), (1, 8))),
        "cotangent": centred(key_of[1], (GROUPS, GROUP_TOK, D), 1.0, 6.0, ((0, 4), (1, 8))),
        "w_query": centred(key_of[2], (D * Q_WIDTH,), (D // 2) ** -0.5, 0.25, ((0, 32),)),
        "w_key": centred(key_of[3], (D * KV_WIDTH,), (D // 2) ** -0.5, 0.25, ((0, 32),)),
        "w_value": centred(key_of[4], (D * KV_WIDTH,), D ** -0.5, 0.1875, ((0, 32),)),
        "w_output": centred(key_of[5], (Q_WIDTH * D,), (Q_WIDTH // 16) ** -0.5, 0.75, ((0, 32),)),
        "w_gate": centred(key_of[6], (D * FF,), D ** -0.5, 0.1875, ((0, 32),)),
        "w_up": centred(key_of[7], (D * FF,), D ** -0.5, 0.1875, ((0, 32),)),
        "w_down": centred(key_of[8], (FF * D,), (FF // 2) ** -0.5, 0.15625, ((0, 32),)),
        "norm_gains": jnp.clip(1.0 + 0.15 * jax.random.normal(key_of[9], (2, D), jnp.float32), 0.25, 1.75).astype(jnp.bfloat16),
        "seq_lengths": draw_seq_lengths(jax.random.fold_in(key_of[12], 71), 0),
        "block_order": draw_block_order(jax.random.fold_in(key_of[12], 71), 0),
    }


@jax.custom_vjp
def low(v):
    return lax.optimization_barrier(v.astype(jnp.bfloat16)).astype(jnp.float32)

@jax.custom_vjp
def low_back(v):
    return v

def low_keep(v):
    return (low(v), None)

def low_pass(kept, grad):
    return (grad,)

def back_keep(v):
    return (v, None)

def back_low(kept, grad):
    return (low(grad),)
low.defvjp(low_keep, low_pass)
low_back.defvjp(back_keep, back_low)

def product(left, right):
    return jnp.dot(left, right, precision=lax.Precision.HIGHEST)

def rms_scale(values):
    return lax.rsqrt(lax.optimization_barrier(jnp.mean(values * values, axis=-1, keepdims=True)) + 1e-05)

def frequencies():
    half_dim = HEAD_DIM // 2
    return 10000.0 ** (-(2.0 * jnp.arange(half_dim).astype(jnp.float32)) / HEAD_DIM)

def rotary(values, angles):
    half_dim = values.shape[-1] // 2
    first = values[..., :half_dim]
    second = values[..., half_dim:]
    cosine = jnp.cos(angles)[:, None, :]
    sine = jnp.sin(angles)[:, None, :]
    return jnp.concatenate([first * cosine - second * sine, second * cosine + first * sine], axis=-1)

def token_tables(lengths, arrangement):
    ends = jnp.cumsum(lengths).astype(jnp.int32)
    starts = (ends - lengths).astype(jnp.int32)
    logical = (arrangement[:, None] * BLOCK + jnp.arange(BLOCK, dtype=jnp.int32)[None, :]).reshape(-1).astype(jnp.int32)
    document = lax.optimization_barrier(jnp.sum((logical[:, None] >= ends[None, :]).astype(jnp.int32), axis=1)).astype(jnp.int32)
    chosen = document[:, None] == jnp.arange(SEQS, dtype=jnp.int32)[None, :]
    offset = lax.optimization_barrier(jnp.sum(jnp.where(chosen, starts[None, :], 0), axis=1)).astype(jnp.int32)
    return (logical, document, (logical - offset).astype(jnp.int32))

def attention(queries, keys, values, logical, document):
    total = queries.shape[0]
    row_block = min(512, total)
    count = total // row_block
    repeat = HEADS // KV_HEADS
    score_scale = HEAD_DIM ** (-0.5)
    grouped = queries.reshape(count, row_block, KV_HEADS, repeat, HEAD_DIM)

    def one_block(block_item):
        block_query, block_logical, block_document = block_item
        scores = jnp.einsum('tgrd,ngd->grtn', block_query, keys, precision=lax.Precision.HIGHEST) * score_scale
        scores = low_back(scores)
        allowed = (block_document[:, None] == document[None, :]) & (logical[None, :] <= block_logical[:, None])
        scores = jnp.where(allowed, scores, -1e+30)
        top_score = lax.optimization_barrier(jnp.max(scores, axis=-1, keepdims=True))
        expo = jnp.exp(scores - top_score)
        probs = low(expo / lax.optimization_barrier(jnp.sum(expo, axis=-1, keepdims=True)))
        mixed = jnp.einsum('grtn,ngd->tgrd', probs, values, precision=lax.Precision.HIGHEST)
        return low(low_back(mixed)).reshape(row_block, HEADS * HEAD_DIM)
    result = lax.map(jax.checkpoint(one_block), (grouped, logical.reshape(count, row_block), document.reshape(count, row_block)))
    return result.reshape(total, HEADS * HEAD_DIM)

def group_forward(tokens, weights, gains, logical, document, position):
    w_query, w_key, w_value, w_output, w_gate, w_up, w_down = weights
    total = tokens.shape[0]
    angles = position.astype(jnp.float32)[:, None] * frequencies()[None, :]
    normed = low(tokens * rms_scale(tokens) * gains[0])
    query_proj = low_back(product(normed, w_query)).reshape(total, HEADS, HEAD_DIM)
    queries = low(rotary(query_proj, angles)).reshape(total, KV_HEADS, HEADS // KV_HEADS, HEAD_DIM)
    key_proj = low_back(product(normed, w_key)).reshape(total, KV_HEADS, HEAD_DIM)
    keys = low(rotary(key_proj, angles))
    values = low(low_back(product(normed, w_value))).reshape(total, KV_HEADS, HEAD_DIM)
    attended = attention(queries, keys, values, logical, document)
    hidden = tokens + low_back(product(attended, w_output))
    normed_two = low(hidden * rms_scale(hidden) * gains[1])
    gate = low_back(product(normed_two, w_gate))
    upward = low_back(product(normed_two, w_up))
    inner = low(jax.nn.silu(gate) * upward)
    return hidden + low_back(product(inner, w_down))

def reference(tokens_in, cotangent, w_query, w_key, w_value, w_output, w_gate, w_up, w_down, norm_gains, seq_lengths, block_order):
    logical, document, position = jax.vmap(token_tables)(seq_lengths, block_order)
    shapes = ((D, Q_WIDTH), (D, KV_WIDTH), (D, KV_WIDTH), (Q_WIDTH, D), (D, FF), (D, FF), (FF, D))
    flats = (w_query, w_key, w_value, w_output, w_gate, w_up, w_down)
    weights = tuple((flat.astype(jnp.float32).reshape(shape_pair) for flat, shape_pair in zip(flats, shapes)))
    gains = norm_gains.astype(jnp.float32)
    tokens = tokens_in.astype(jnp.float32)

    def forward(inputs, weight_set, gain_set):

        def per_group(group_item):
            return group_forward(group_item[0], weight_set, gain_set, group_item[1], group_item[2], group_item[3])
        return lax.map(per_group, (inputs, logical, document, position))
    block_out, pullback = jax.vjp(forward, tokens, weights, gains)
    grad_tokens, grad_weights, grad_gain_set = pullback(cotangent.astype(jnp.float32))
    flat_grads = tuple((grad.reshape(-1) for grad in grad_weights))
    return (block_out, grad_tokens, flat_grads[0], flat_grads[1], flat_grads[2], flat_grads[3], flat_grads[4], flat_grads[5], flat_grads[6], grad_gain_set)
```

```python
import jax
import jax.numpy as jnp
from jax import lax
from jax.sharding import PartitionSpec as P

D = 960
HEADS = 15
KV_HEADS = 5
HEAD_DIM = 64
FF = 2560
BLOCK = 128
SEQS = 3
Q_WIDTH = 960
KV_WIDTH = 320


def rms_scale(values):
    return lax.rsqrt(jnp.mean(values * values, axis=-1, keepdims=True) + 1e-05)


def frequencies():
    half_dim = HEAD_DIM // 2
    return 10000.0 ** (-(2.0 * jnp.arange(half_dim).astype(jnp.float32)) / HEAD_DIM)


def rotary(values, angles):
    half_dim = values.shape[-1] // 2
    first = values[..., :half_dim]
    second = values[..., half_dim:]
    cosine = jnp.cos(angles)[:, None, :]
    sine = jnp.sin(angles)[:, None, :]
    return jnp.concatenate(
        [first * cosine - second * sine, second * cosine + first * sine], axis=-1
    )


def token_tables(lengths, arrangement):
    ends = jnp.cumsum(lengths)
    starts = ends - lengths
    logical = (arrangement[:, None] * BLOCK + jnp.arange(BLOCK, dtype=jnp.int32)[None, :]).reshape(
        -1
    )
    document = jnp.sum((logical[:, None] >= ends[None, :]).astype(jnp.int32), axis=1)
    chosen = document[:, None] == jnp.arange(SEQS, dtype=jnp.int32)[None, :]
    offset = jnp.sum(jnp.where(chosen, starts[None, :], 0), axis=1)
    return (logical, document, logical - offset)


def matmul(left, right):
    return jnp.dot(left, right, preferred_element_type=jnp.float32)


def outer_sum(left, right):
    return lax.dot_general(
        left, right, (((0,), (0,)), ((), ())), preferred_element_type=jnp.float32
    )


def back_dot(grad_rows, weight):
    return lax.dot_general(
        grad_rows, weight, (((1,), (1,)), ((), ())), preferred_element_type=jnp.float32
    )


def norm_back(grad_normed, base_normed, inv_scale, gain_row):
    scaled = grad_normed * gain_row
    grad_rows = inv_scale * (
        scaled - base_normed * jnp.mean(scaled * base_normed, axis=-1, keepdims=True)
    )
    return (grad_rows, jnp.sum(grad_normed * base_normed, axis=0))


def local(
    tokens_in,
    cotangent,
    w_query,
    w_key,
    w_value,
    w_output,
    w_gate,
    w_up,
    w_down,
    norm_gains,
    seq_lengths,
    block_order,
):
    row_count = tokens_in.shape[1]
    repeat = HEADS // KV_HEADS
    score_scale = HEAD_DIM ** (-0.5)
    shapes = ((D, Q_WIDTH), (D, KV_WIDTH), (D, KV_WIDTH), (Q_WIDTH, D), (D, FF), (D, FF), (FF, D))
    axes = ("dp", "ctx")
    by_rows = w_query.shape[0] % D == 0
    if by_rows:
        rows = w_query.shape[0] // D
        local_one = jnp.concatenate(
            [w.reshape(rows, -1) for w in (w_query, w_key, w_value, w_output)], axis=1
        )
        whole_one = lax.all_gather(local_one.reshape(-1), axes, axis=0, tiled=True).reshape(D, -1)
        full_query = whole_one[:, :Q_WIDTH]
        full_key = whole_one[:, Q_WIDTH : Q_WIDTH + KV_WIDTH]
        full_value = whole_one[:, Q_WIDTH + KV_WIDTH : Q_WIDTH + 2 * KV_WIDTH]
        full_output = whole_one[:, Q_WIDTH + 2 * KV_WIDTH :]
    else:
        full_query, full_key, full_value, full_output = tuple(
            lax.all_gather(w, axes, axis=0, tiled=True).reshape(pair)
            for w, pair in zip((w_query, w_key, w_value, w_output), shapes[:4])
        )
    lengths = seq_lengths[0]
    arrangement = block_order[0]
    logical_all, document_all, position_all = token_tables(lengths, arrangement)
    group_total = logical_all.shape[0]
    block_total = arrangement.shape[0]
    first_row = lax.axis_index("ctx") * row_count
    own_logical = lax.dynamic_slice_in_dim(logical_all, first_row, row_count)
    own_document = lax.dynamic_slice_in_dim(document_all, first_row, row_count)
    own_position = lax.dynamic_slice_in_dim(position_all, first_row, row_count)
    angles = own_position.astype(jnp.float32)[:, None] * frequencies()[None, :]
    low_block = jnp.min(own_logical - own_position) // BLOCK
    high_block = jnp.max(own_logical) // BLOCK + 1
    ends = jnp.cumsum(lengths)
    packed_index = jnp.arange(group_total, dtype=jnp.int32)
    packed_document = jnp.sum((packed_index[:, None] >= ends[None, :]).astype(jnp.int32), axis=1)
    block_ids = jnp.arange(block_total, dtype=jnp.int32)
    stored_of_packed = jnp.sum(
        jnp.where(arrangement[None, :] == block_ids[:, None], block_ids[None, :], 0), axis=1
    )
    tokens = tokens_in[0].astype(jnp.float32)
    gains = norm_gains.astype(jnp.float32)
    inv_one = rms_scale(tokens)
    base_one = tokens * inv_one
    normed = (base_one * gains[0]).astype(jnp.bfloat16)
    query_proj = matmul(normed, full_query).reshape(row_count, HEADS, HEAD_DIM)
    queries = (
        rotary(query_proj, angles)
        .astype(jnp.bfloat16)
        .reshape(row_count, KV_HEADS, repeat, HEAD_DIM)
    )
    key_proj = matmul(normed, full_key).reshape(row_count, KV_HEADS, HEAD_DIM)
    keys_own = rotary(key_proj, angles).astype(jnp.bfloat16).reshape(row_count, KV_WIDTH)
    values_own = matmul(normed, full_value).astype(jnp.bfloat16)
    all_pairs = lax.all_gather(
        jnp.concatenate([keys_own, values_own], axis=1), "ctx", axis=0, tiled=True
    )
    if by_rows:
        local_two = jnp.concatenate([w.reshape(rows, -1) for w in (w_gate, w_up, w_down)], axis=1)
        local_two, all_pairs = lax.optimization_barrier((local_two.reshape(-1), all_pairs))
        whole_two = lax.all_gather(local_two, axes, axis=0, tiled=True).reshape(D, -1)
        full_gate = whole_two[:, :FF]
        full_up = whole_two[:, FF : 2 * FF]
        full_down = whole_two[:, 2 * FF :].reshape(FF, D)
    else:
        full_gate, full_up, full_down = tuple(
            lax.all_gather(w, axes, axis=0, tiled=True).reshape(pair)
            for w, pair in zip((w_gate, w_up, w_down), shapes[4:])
        )
    packed_pairs = jnp.take(
        all_pairs.reshape(block_total, BLOCK, 2 * KV_WIDTH), stored_of_packed, axis=0
    ).reshape(group_total, 2 * KV_WIDTH)
    packed_keys = packed_pairs[:, :KV_WIDTH].reshape(group_total, KV_HEADS, HEAD_DIM)
    packed_values = packed_pairs[:, KV_WIDTH:].reshape(group_total, KV_HEADS, HEAD_DIM)

    def block_scores(block_index):
        start = block_index * BLOCK
        key_piece = lax.dynamic_slice_in_dim(packed_keys, start, BLOCK, 0)
        value_piece = lax.dynamic_slice_in_dim(packed_values, start, BLOCK, 0)
        key_logical = start + jnp.arange(BLOCK, dtype=jnp.int32)
        key_document = lax.dynamic_slice_in_dim(packed_document, start, BLOCK, 0)
        scores = (
            jnp.einsum("tgrd,ngd->grtn", queries, key_piece, preferred_element_type=jnp.float32)
            * score_scale
        )
        allowed = (own_document[:, None] == key_document[None, :]) & (
            key_logical[None, :] <= own_logical[:, None]
        )
        return (scores, allowed, key_piece, value_piece)

    def pass_total(block_index, state_pair):
        top_score, running = state_pair
        scores, allowed, _, _ = block_scores(block_index)
        scores = jnp.where(allowed, scores, -1e30)
        new_top = jnp.maximum(top_score, jnp.max(scores, axis=-1))
        expo = jnp.where(allowed, jnp.exp(scores - new_top[..., None]), 0.0)
        running = running * jnp.exp(top_score - new_top) + jnp.sum(expo, axis=-1)
        return (new_top, running)

    start_top = jnp.full((KV_HEADS, repeat, row_count), -1e30, jnp.float32)
    start_total = jnp.zeros((KV_HEADS, repeat, row_count), jnp.float32)
    top_score, running = lax.fori_loop(low_block, high_block, pass_total, (start_top, start_total))
    log_total = top_score + jnp.log(running)

    def pass_mix(block_index, accumulated):
        scores, allowed, _, value_piece = block_scores(block_index)
        probs = jnp.where(allowed, jnp.exp(scores - log_total[..., None]), 0.0).astype(jnp.bfloat16)
        return accumulated + jnp.einsum(
            "grtn,ngd->tgrd", probs, value_piece, preferred_element_type=jnp.float32
        )

    start_mix = jnp.zeros((row_count, KV_HEADS, repeat, HEAD_DIM), jnp.float32)
    mixed = lax.fori_loop(low_block, high_block, pass_mix, start_mix)
    attended = mixed.reshape(row_count, Q_WIDTH).astype(jnp.bfloat16)
    hidden = tokens + matmul(attended, full_output)
    inv_two = rms_scale(hidden)
    base_two = hidden * inv_two
    normed_two = (base_two * gains[1]).astype(jnp.bfloat16)
    gate = matmul(normed_two, full_gate)
    upward = matmul(normed_two, full_up)
    sigma = jax.nn.sigmoid(gate)
    inner = (gate * sigma * upward).astype(jnp.bfloat16)
    block_out = hidden + matmul(inner, full_down)
    back_query, back_key, back_value, back_output, back_gate, back_up, back_down = (
        full_query,
        full_key,
        full_value,
        full_output,
        full_gate,
        full_up,
        full_down,
    )
    grad_out = cotangent[0].astype(jnp.float32)
    grad_low = cotangent[0]
    grad_down = outer_sum(inner, grad_low)
    grad_inner = back_dot(grad_low, back_down)
    grad_gate_act = (grad_inner * upward * sigma * (1.0 + gate * (1.0 - sigma))).astype(
        jnp.bfloat16
    )
    grad_up_act = (grad_inner * gate * sigma).astype(jnp.bfloat16)
    grad_gate = outer_sum(normed_two, grad_gate_act)
    grad_up = outer_sum(normed_two, grad_up_act)
    grad_normed_two = back_dot(grad_gate_act, back_gate) + back_dot(grad_up_act, back_up)
    grad_hidden_norm, gain_two = norm_back(grad_normed_two, base_two, inv_two, gains[1])
    grad_hidden = grad_out + grad_hidden_norm
    hidden_low = grad_hidden.astype(jnp.bfloat16)
    grad_output = outer_sum(attended, hidden_low)
    grad_attended = back_dot(hidden_low, back_output).astype(jnp.bfloat16)
    def flat_low(parts):
        return jnp.concatenate([part.astype(jnp.bfloat16).reshape(-1) for part in parts])

    low_two, low_down, grad_attended = lax.optimization_barrier(
        (flat_low((grad_gate, grad_up)), flat_low((grad_down,)), grad_attended)
    )
    sum_down = lax.psum(low_down, axes)
    grad_attended_heads = grad_attended.reshape(row_count, KV_HEADS, repeat, HEAD_DIM)
    delta = jnp.sum(grad_attended_heads.astype(jnp.float32) * mixed, axis=-1).transpose(1, 2, 0)

    def back_block(block_index, carry):
        grad_queries, grad_key_full, grad_value_full = carry
        scores, allowed, key_piece, value_piece = block_scores(block_index)
        probs = jnp.where(allowed, jnp.exp(scores - log_total[..., None]), 0.0)
        grad_probs = jnp.einsum(
            "tgrd,ngd->grtn", grad_attended_heads, value_piece, preferred_element_type=jnp.float32
        )
        grad_scores = (probs * (grad_probs - delta[..., None])).astype(jnp.bfloat16)
        grad_queries = (
            grad_queries
            + jnp.einsum(
                "grtn,ngd->tgrd", grad_scores, key_piece, preferred_element_type=jnp.float32
            )
            * score_scale
        )
        grad_key_piece = (
            jnp.einsum("grtn,tgrd->ngd", grad_scores, queries, preferred_element_type=jnp.float32)
            * score_scale
        )
        grad_value_piece = jnp.einsum(
            "grtn,tgrd->ngd",
            probs.astype(jnp.bfloat16),
            grad_attended_heads,
            preferred_element_type=jnp.float32,
        )
        start = block_index * BLOCK
        grad_key_full = lax.dynamic_update_slice_in_dim(
            grad_key_full, grad_key_piece.reshape(BLOCK, KV_WIDTH), start, 0
        )
        grad_value_full = lax.dynamic_update_slice_in_dim(
            grad_value_full, grad_value_piece.reshape(BLOCK, KV_WIDTH), start, 0
        )
        return (grad_queries, grad_key_full, grad_value_full)

    zero_rows = jnp.zeros((group_total, KV_WIDTH), jnp.float32)
    grad_queries, grad_key_full, grad_value_full = lax.fori_loop(
        low_block,
        high_block,
        back_block,
        (jnp.zeros((row_count, KV_HEADS, repeat, HEAD_DIM), jnp.float32), zero_rows, zero_rows),
    )
    grad_pairs = jnp.concatenate([grad_key_full, grad_value_full], axis=1).astype(jnp.bfloat16)
    grad_pairs = jnp.take(
        grad_pairs.reshape(block_total, BLOCK, 2 * KV_WIDTH), arrangement, axis=0
    ).reshape(group_total, 2 * KV_WIDTH)
    grad_pairs, sum_down = lax.optimization_barrier((grad_pairs, sum_down))
    own_pairs = lax.psum_scatter(grad_pairs, "ctx", scatter_dimension=0, tiled=True)
    own_pairs, low_two = lax.optimization_barrier((own_pairs, low_two))
    sum_two = lax.psum(low_two, axes)
    grad_keys_own = own_pairs[:, :KV_WIDTH].astype(jnp.float32)
    grad_values_own = own_pairs[:, KV_WIDTH:].astype(jnp.float32)
    grad_query_proj = (
        rotary(grad_queries.reshape(row_count, HEADS, HEAD_DIM), -angles)
        .reshape(row_count, Q_WIDTH)
        .astype(jnp.bfloat16)
    )
    grad_key_proj = (
        rotary(grad_keys_own.reshape(row_count, KV_HEADS, HEAD_DIM), -angles)
        .reshape(row_count, KV_WIDTH)
        .astype(jnp.bfloat16)
    )
    grad_value_proj = grad_values_own.astype(jnp.bfloat16)
    grad_query = outer_sum(normed, grad_query_proj)
    grad_key = outer_sum(normed, grad_key_proj)
    grad_value = outer_sum(normed, grad_value_proj)
    grad_normed = (
        back_dot(grad_query_proj, back_query)
        + back_dot(grad_key_proj, back_key)
        + back_dot(grad_value_proj, back_value)
    )
    grad_input_norm, gain_one = norm_back(grad_normed, base_one, inv_one, gains[0])
    grad_input = grad_hidden + grad_input_norm
    rank = lax.axis_index("dp") * lax.axis_size("ctx") + lax.axis_index("ctx")

    def own_parts(summed, sizes):
        base, taken = 0, []
        for size in sizes:
            taken.append(
                lax.dynamic_slice_in_dim(summed, base + rank * size, size).astype(jnp.float32)
            )
            base += size * device_count
        return tuple(taken)

    device_count = lax.axis_size("dp") * lax.axis_size("ctx")
    own_gate, own_up = own_parts(sum_two, (w_gate.shape[0], w_up.shape[0]))
    (own_down,) = own_parts(sum_down, (w_down.shape[0],))
    low_one = flat_low((grad_query, grad_key, grad_value, grad_output, gain_one, gain_two))
    low_one, own_gate = lax.optimization_barrier((low_one, own_gate))
    sum_one = lax.psum(low_one, axes)
    own_query, own_key, own_value, own_output = own_parts(
        sum_one, (w_query.shape[0], w_key.shape[0], w_value.shape[0], w_output.shape[0])
    )
    grad_gains = sum_one[-2 * D :].astype(jnp.float32).reshape(2, D)
    return (
        block_out[None],
        grad_input[None],
        own_query,
        own_key,
        own_value,
        own_output,
        own_gate,
        own_up,
        own_down,
        grad_gains,
    )


def solution(mesh):
    return jax.shard_map(
        local,
        mesh=mesh,
        in_specs=(
            P("dp", "ctx", None),
            P("dp", "ctx", None),
            P(("dp", "ctx")),
            P(("dp", "ctx")),
            P(("dp", "ctx")),
            P(("dp", "ctx")),
            P(("dp", "ctx")),
            P(("dp", "ctx")),
            P(("dp", "ctx")),
            P(),
            P("dp", None),
            P("dp", None),
        ),
        out_specs=(
            P("dp", "ctx", None),
            P("dp", "ctx", None),
            P(("dp", "ctx")),
            P(("dp", "ctx")),
            P(("dp", "ctx")),
            P(("dp", "ctx")),
            P(("dp", "ctx")),
            P(("dp", "ctx")),
            P(("dp", "ctx")),
            P(),
        ),
        check_vma=False,
    )
```
